32 devices in a mesh: groups: 2 (over y), ctx: 8 (over z, x), head: 2 (over core).
Axes of the slice: x: 2, y: 2, z: 4, core: 2. Of those that a mesh axis runs over, the one named last changes fastest.
Arguments:
- query_latent: bfloat16 [16, 64, 512], P(('groups', 'ctx'), 'head'), parts along dimension 0, may hold values from -16 to 16
- query_rope: bfloat16 [16, 64, 64], P(('groups', 'ctx'), 'head'), parts along dimension 0, may hold values from -6 to 6
- cache_latent: bfloat16 [4096, 512], P(('groups', 'ctx')), parts along dimension 0, may hold values from -4 to 4
- cache_rope: bfloat16 [4096, 64], P(('groups', 'ctx')), parts along dimension 0, may hold values from -6 to 6
- value_up: bfloat16 [64, 512, 128], P('head', 'ctx'), may hold values from -0.25 to 0.25
- out_proj: bfloat16 [128, 64, 7168], P('ctx', 'head'), may hold values from -0.25 to 0.25
Outputs:
- attended: bfloat16 [16, 7168], P(('groups', 'ctx'), 'head'), parts along dimension 0
The draws below stay inside these ranges and needn't reach their ends.
There are 2 independent parts, one for each index of `groups`. The reference program is written for one: setup_inputs(seed, part) draws one part's arguments, and reference() takes and returns one part's arrays. A program takes and returns all parts, laid end to end along the dimension named above; an argument that names none is the same for every part. Nothing has to cross between parts.
All inputs are finite; a program needn't handle non-finite values.
Results may differ from the reference program's by a relative error of at most 0.0075.
Values may be sent and summed in bfloat16 or wider, within the bound.
A program may use at most 64 MiB of HBM per device.

```python
import jax
import jax.numpy as jnp
from jax import lax

D = 7168
HEADS = 64
LAT = 512
ROPE = 64
NOPE = 128
VD = 128
SPAN = 8
PREFIX = 2048


def row_scales(key, low, high):
    spread = jax.random.uniform(key, (SPAN, HEADS, 1), jnp.float32, jnp.log(low), jnp.log(high))
    return jnp.exp(spread)


def draw_cache_latent(key, part):
    values = jax.random.normal(jax.random.fold_in(key, 9), (PREFIX, LAT), jnp.float32)
    return jnp.clip(values, -4.0, 4.0).astype(jnp.bfloat16)


def draw_query_latent(key, part):
    own_key = jax.random.fold_in(key, 5)
    scale_key = jax.random.fold_in(key, 7)
    scales = row_scales(scale_key, 0.5, 5.0)
    values = jnp.clip(jax.random.normal(own_key, (SPAN, HEADS, LAT), jnp.float32) * scales, -16.0, 16.0)
    return values.astype(jnp.bfloat16)


def shard_levels(key, dims, pieces, least, largest):
    def one(position, blocks):
        steps = jax.random.uniform(jax.random.fold_in(jax.random.fold_in(key, 6), position), (blocks,), jnp.float32, least / len(pieces), largest / len(pieces))
        return jnp.repeat(jnp.exp(steps), dims[position] // blocks).reshape((-1,) + (1,) * (len(dims) - position - 1))

    gain = one(*pieces[0])
    for cut in pieces[1:]:
        gain = gain * one(*cut)
    return gain


def centred(stream_key, dims, scale, reach, shards=(), kind=jnp.bfloat16):
    drawn = jax.random.normal(stream_key, dims, jnp.float32) * scale
    if len(shards) > 0:
        drawn = shard_levels(stream_key, dims, shards, -0.22, 0.18) * drawn
    return jnp.clip(drawn, min=-reach, max=reach).astype(kind)


def setup_inputs(seed: int = 0, part: int = 0) -> dict:
    seeds = jax.random.split(jax.random.key(seed), 7)
    own_keys = jax.random.split(jax.random.fold_in(seeds[6], part), 7)
    return {
        "query_latent": draw_query_latent(jax.random.fold_in(jax.random.fold_in(seeds[6], part), 71), part),
        "query_rope": centred(own_keys[1], (SPAN, HEADS, ROPE), 1.0, 6.0, ((0, 8), (1, 2))),
        "cache_latent": draw_cache_latent(jax.random.fold_in(jax.random.fold_in(seeds[6], part), 71), part),
        "cache_rope": centred(own_keys[3], (PREFIX, ROPE), 1.0, 6.0, ((0, 8),)),
        "value_up": centred(seeds[4], (HEADS, LAT, VD), LAT ** -0.5, 0.25, ((0, 2), (1, 8))),
        "out_proj": centred(seeds[5], (VD, HEADS, D), (HEADS * VD // 16) ** -0.5, 0.25, ((0, 8), (1, 2))),
    }


def reference(query_latent, query_rope, cache_latent, cache_rope, value_up, out_proj):
    score_scale = (NOPE + ROPE) ** -0.5

    def one_head(inputs):
        latent_query, rotary_query, value_matrix = inputs
        scores = (jnp.dot(latent_query, cache_latent.T, preferred_element_type=jnp.float32)
                  + jnp.dot(rotary_query, cache_rope.T, preferred_element_type=jnp.float32)) * score_scale
        peak_score = jnp.max(scores, axis=1, keepdims=True)
        raised = jnp.exp(scores - peak_score)
        totals = jnp.sum(raised, axis=1, keepdims=True)
        weights = raised.astype(jnp.bfloat16)
        latent_out = jnp.dot(weights, cache_latent, preferred_element_type=jnp.float32)
        projected = jnp.dot(latent_out, value_matrix.astype(jnp.float32), precision=lax.Precision.HIGHEST)
        return (projected / totals).astype(jnp.bfloat16)

    heads_out = lax.map(one_head, (jnp.transpose(query_latent, (1, 0, 2)), jnp.transpose(query_rope, (1, 0, 2)), value_up))
    flattened = jnp.transpose(heads_out, (1, 0, 2)).reshape(SPAN, HEADS * VD)
    projection = jnp.transpose(out_proj, (1, 0, 2)).reshape(HEADS * VD, D)
    return jnp.dot(flattened, projection, preferred_element_type=jnp.float32).astype(jnp.bfloat16)
```

```python
import functools

import jax
import jax.numpy as jnp
from jax import lax
from jax.experimental import pallas as pl
from jax.experimental.pallas import tpu as pltpu
from jax.sharding import PartitionSpec as P

ROPE = 64
NOPE = 128
SCALE = (NOPE + ROPE) ** (-0.5)
F32 = jnp.float32
BF16 = jnp.bfloat16
MESH = pl.DeviceIdType.MESH
STAT = 16


def contract(a, b, da, db):
    return lax.dot_general(a, b, (((da,), (db,)), ((), ())), preferred_element_type=F32)


def kernel(
    n, ql, qr, cl, cr, vu, wo, out,
    qlb, qrb, clb, crb, vub, wob,
    lat_send, lat_recv, comb, proj, pr_send, pr_recv, att, at_send, at_recv,
    local_sem, q_send, q_recv, c_send, c_recv, l_send, l_recv, p_send, p_recv, a_send, a_recv,
):
    me = lax.axis_index("ctx")
    hd = lax.axis_index("head")
    half = n // 2
    z = me // 2
    x = me % 2
    partner = 2 * z + 1 - x
    heads = ql.shape[1]
    tokens = cl.shape[0]
    share = vu.shape[1]
    cols = lat_send.shape[2]
    vshare = pr_send.shape[1]
    rows = proj.shape[0]
    chunks = out.shape[1] // 128
    pad = at_send.shape[2]

    own = pl.ds(0, tokens)
    local = [
        pltpu.make_async_copy(cl, clb.at[own], local_sem.at[0]),
        pltpu.make_async_copy(cr, crb.at[own], local_sem.at[1]),
        pltpu.make_async_copy(ql.at[0], qlb.at[z], local_sem.at[2]),
        pltpu.make_async_copy(qr.at[0], qrb.at[z], local_sem.at[3]),
        pltpu.make_async_copy(vu, vub, local_sem.at[4]),
        pltpu.make_async_copy(wo, wob, local_sem.at[5]),
    ]
    for copy in local:
        copy.start()

    barrier = pltpu.get_barrier_semaphore()
    for e in range(2):
        for d in range(n):
            if e or d:
                pl.semaphore_signal(
                    barrier, inc=1, device_id={"ctx": (me + d) % n, "head": (hd + e) % 2},
                    device_id_type=MESH,
                )
    pl.semaphore_wait(barrier, 2 * n - 1)

    part = tokens // 2
    mine = pl.ds(pl.multiple_of(hd * part, part), part)
    there = pl.ds(pl.multiple_of(tokens + hd * part, part), part)
    cache = [
        pltpu.make_async_remote_copy(
            src.at[mine], dst.at[there], c_send.at[k], c_recv.at[k],
            device_id={"ctx": partner}, device_id_type=MESH,
        )
        for k, (src, dst) in enumerate(((cl, clb), (cr, crb)))
    ]
    queries = []
    for d in range(1, half):
        peer = 2 * ((z + d) % half) + x
        for k, (src, dst) in enumerate(((ql, qlb), (qr, qrb))):
            queries.append(
                pltpu.make_async_remote_copy(
                    src.at[0], dst.at[z], q_send.at[k, d], q_recv.at[k, d],
                    device_id={"ctx": peer}, device_id_type=MESH,
                )
            )
    for copy in cache + queries:
        copy.start()

    for copy in local[:4]:
        copy.wait()
    for copy in cache:
        copy.wait_recv()
    swap = [
        pltpu.make_async_remote_copy(
            dst.at[there], dst.at[there], c_send.at[2 + k], c_recv.at[2 + k],
            device_id={"head": 1 - hd}, device_id_type=MESH,
        )
        for k, dst in enumerate((clb, crb))
    ]
    for copy in swap:
        copy.start()
    for copy in queries:
        copy.wait_recv()

    q = qlb[...].reshape(cols, qlb.shape[2])
    r = qrb[...].reshape(cols, qrb.shape[2])
    first = contract(clb[0:tokens], q, 1, 1) + contract(crb[0:tokens], r, 1, 1)
    for copy in swap:
        copy.wait_recv()
    second = contract(clb[tokens : 2 * tokens], q, 1, 1) + contract(crb[tokens : 2 * tokens], r, 1, 1)
    scores = jnp.concatenate([first, second], axis=0) * SCALE
    peak = jnp.max(scores, axis=0, keepdims=True).astype(BF16).astype(F32)
    raised = jnp.exp(scores - peak)
    total = jnp.sum(raised, axis=0, keepdims=True)
    latent = contract(clb[...], raised.astype(BF16), 0, 0)
    high = total.astype(BF16).astype(F32)
    row = lax.broadcasted_iota(jnp.int32, (STAT, cols), 0)
    stats = jnp.where(
        row == 0, peak, jnp.where(row == 1, high, jnp.where(row == 2, total - high, 0.0))
    ).astype(BF16)
    for j in range(n):
        lat_send[j, 0:share, :] = latent[j * share : (j + 1) * share].astype(BF16)
        lat_send[j, share : share + STAT, :] = stats

    def exchange(send, recv, send_sem, recv_sem):
        copies = []
        for d in range(1, n):
            peer = (me + d) % n
            copy = pltpu.make_async_remote_copy(
                send.at[peer], recv.at[me], send_sem.at[d], recv_sem.at[d],
                device_id={"ctx": peer}, device_id_type=MESH,
            )
            copy.start()
            copies.append(copy)
        recv[me] = send[me]
        for copy in copies:
            copy.wait_recv()
        return copies

    lat_copies = exchange(lat_send, lat_recv, l_send, l_recv)

    sides = []
    for side in range(2):
        blocks = [lat_recv[2 * k + side].astype(F32) for k in range(half)]
        peaks = [b[share : share + 1] for b in blocks]
        top = functools.reduce(jnp.maximum, peaks)
        factors = [jnp.exp(p - top) for p in peaks]
        whole = sum(f * (b[share + 1 : share + 2] + b[share + 2 : share + 3]) for f, b in zip(factors, blocks))
        sides.append(sum(f * b[0:share] for f, b in zip(factors, blocks)) / whole)
    comb[...] = jnp.concatenate(sides, axis=1).T

    local[4].wait()
    for h in range(heads):
        lhs = comb[pl.ds(h, n, stride=heads), :].astype(BF16)
        proj[pl.ds(h, n, stride=heads), :] = jnp.dot(lhs, vub[h], preferred_element_type=F32)
    flipped = proj[...].T
    for j in range(n):
        pr_send[j] = flipped[j * vshare : (j + 1) * vshare].astype(BF16)
    pr_copies = exchange(pr_send, pr_recv, p_send, p_recv)

    head_out = sum(pr_recv[s].astype(F32) for s in range(n)).astype(BF16)
    wide = vshare * heads
    spread = (
        lax.broadcasted_iota(jnp.int32, (vshare, wide), 1) // heads
        == lax.broadcasted_iota(jnp.int32, (vshare, wide), 0)
    ).astype(F32).astype(BF16)
    copied = contract(head_out, spread, 0, 0)
    keep = (
        lax.broadcasted_iota(jnp.int32, (rows, wide), 1) % heads
        == lax.broadcasted_iota(jnp.int32, (rows, wide), 0) % heads
    )
    lhs = jnp.sum(jnp.where(keep, copied, 0.0).reshape(n, heads, wide), axis=1).astype(BF16)

    local[5].wait()
    for k in range(2):
        for c in range(chunks):
            at = (k * chunks + c) * 128
            att[pl.ds(k * n * pad + c, n, stride=pad), :] = jnp.dot(
                lhs, wob[:, at : at + 128], preferred_element_type=F32
            )
        for c in range(chunks, pad):
            att[pl.ds(k * n * pad + c, n, stride=pad), :] = jnp.zeros((n, 128), F32)
    for k in range(2):
        for j in range(n):
            slot = (j % 2) * half + j // 2
            at = (k * n + slot) * pad
            at_send[k, j] = att[at : at + pad, :].astype(BF16)

    at_copies = []
    for e in (1, 0):
        for d in range(n):
            if e or d:
                peer = (me + d) % n
                other = (hd + e) % 2
                copy = pltpu.make_async_remote_copy(
                    at_send.at[other, peer], at_recv.at[hd, me], a_send.at[e, d], a_recv.at[e, d],
                    device_id={"ctx": peer, "head": other}, device_id_type=MESH,
                )
                copy.start()
                at_copies.append(copy)
    at_recv[hd, me] = at_send[hd, me]
    for copy in at_copies:
        copy.wait_recv()
    result = sum(at_recv[k, s].astype(F32) for k in range(2) for s in range(n)).astype(BF16)
    for c in range(chunks):
        out[0:1, c * 128 : (c + 1) * 128] = result[c : c + 1, :]

    for copy in cache + queries + swap + lat_copies + pr_copies + at_copies:
        copy.wait_send()


def fused(n, query_latent, query_rope, cache_latent, cache_rope, value_up, out_proj):
    heads, latent_width = query_latent.shape[1:]
    rotary = query_rope.shape[2]
    tokens = cache_latent.shape[0]
    share, value_width = value_up.shape[1:]
    vshare, _, width = out_proj.shape
    half = n // 2
    cols = half * heads
    rows = n * heads
    mine = width // 2
    pad = -(-(mine // 128) // 16) * 16
    wide = vshare * heads
    dma = pltpu.SemaphoreType.DMA
    any_spec = pl.BlockSpec(memory_space=pl.ANY)
    return pl.pallas_call(
        functools.partial(kernel, n),
        out_shape=jax.ShapeDtypeStruct((1, mine), BF16),
        in_specs=[any_spec] * 6,
        out_specs=pl.BlockSpec(memory_space=pltpu.VMEM),
        scratch_shapes=[
            pltpu.VMEM((half, heads, latent_width), BF16),
            pltpu.VMEM((half, heads, rotary), BF16),
            pltpu.VMEM((2 * tokens, latent_width), BF16),
            pltpu.VMEM((2 * tokens, rotary), BF16),
            pltpu.VMEM(value_up.shape, BF16),
            pltpu.VMEM((wide, width), BF16),
            pltpu.VMEM((n, share + STAT, cols), BF16),
            pltpu.VMEM((n, share + STAT, cols), BF16),
            pltpu.VMEM((rows, share), F32),
            pltpu.VMEM((rows, value_width), F32),
            pltpu.VMEM((n, vshare, rows), BF16),
            pltpu.VMEM((n, vshare, rows), BF16),
            pltpu.VMEM((2 * n * pad, 128), F32),
            pltpu.VMEM((2, n, pad, 128), BF16),
            pltpu.VMEM((2, n, pad, 128), BF16),
            dma((6,)),
            dma((2, half)), dma((2, half)),
            dma((4,)), dma((4,)),
            dma((n,)), dma((n,)),
            dma((n,)), dma((n,)),
            dma((2, n)), dma((2, n)),
        ],
        compiler_params=pltpu.CompilerParams(
            collective_id=0, has_side_effects=True, vmem_limit_bytes=56 * 2**20
        ),
    )(query_latent, query_rope, cache_latent, cache_rope, value_up, out_proj.reshape(wide, width))


def per_device(query_latent, query_rope, cache_latent, cache_rope, value_up, out_proj):
    n = lax.axis_size("ctx")
    if n % 2 == 0 and n <= 16 and value_up.shape[1] % 16 == 0 and out_proj.shape[0] % 16 == 0:
        return fused(n, query_latent, query_rope, cache_latent, cache_rope, value_up, out_proj)
    return plain(query_latent, query_rope, cache_latent, cache_rope, value_up, out_proj)


def plain(query_latent, query_rope, cache_latent, cache_rope, value_up, out_proj):
    score_scale = (NOPE + ROPE) ** (-0.5)
    rows_here, heads_here, latent_width = query_latent.shape
    rotary_width = query_rope.shape[2]
    latent_share, value_width = (value_up.shape[1], value_up.shape[2])
    column_share = out_proj.shape[0]
    per_block = min(8, heads_here)
    block_count = heads_here // per_block
    latent_blocks = jnp.transpose(
        query_latent.reshape(rows_here, block_count, per_block, latent_width), (1, 0, 2, 3)
    )
    rotary_blocks = jnp.transpose(
        query_rope.reshape(rows_here, block_count, per_block, rotary_width), (1, 0, 2, 3)
    )
    value_blocks = value_up.reshape(block_count, per_block, latent_share, value_width)
    column_start = lax.axis_index("ctx") * column_share

    def attend_block(blocks):
        latent_block, rotary_block, value_block = blocks
        gathered_latent, gathered_rotary = (
            lax.all_gather(latent_block, "ctx", axis=0, tiled=True),
            lax.all_gather(rotary_block, "ctx", axis=0, tiled=True),
        )
        scores = (
            jnp.einsum(
                "qhc,kc->qhk", gathered_latent, cache_latent, preferred_element_type=jnp.float32
            )
            + jnp.einsum(
                "qhr,kr->qhk", gathered_rotary, cache_rope, preferred_element_type=jnp.float32
            )
        ) * score_scale
        peaks = jnp.max(scores, axis=2)
        raised = jnp.exp(scores - peaks[:, :, None])
        totals = jnp.sum(raised, axis=2)
        weights = raised.astype(jnp.bfloat16)
        latent_out = jnp.einsum(
            "qhk,kc->qhc", weights, cache_latent, preferred_element_type=jnp.float32
        )
        projected = jnp.einsum(
            "qhc,hcv->qhv",
            latent_out,
            lax.all_gather(value_block, "ctx", axis=1, tiled=True).astype(jnp.float32),
            precision=lax.Precision.HIGHEST,
        )
        peak_all = lax.pmax(peaks, "ctx")
        factor = jnp.exp(peaks - peak_all)
        total_all = lax.psum(totals * factor, "ctx")
        scaled = projected * (factor / total_all)[:, :, None]
        head_full = lax.psum(scaled, "ctx").astype(jnp.bfloat16)
        return lax.dynamic_slice_in_dim(head_full, column_start, column_share, 2)

    column_blocks = lax.map(attend_block, (latent_blocks, rotary_blocks, value_blocks))
    every_row = column_blocks.shape[1]
    head_cols = jnp.transpose(column_blocks, (1, 0, 2, 3)).reshape(
        every_row, heads_here, column_share
    )
    own_rows = lax.psum_scatter(
        jnp.einsum("qhv,vhd->qd", head_cols, out_proj, preferred_element_type=jnp.float32),
        "ctx",
        scatter_dimension=0,
        tiled=True,
    )
    return lax.psum_scatter(own_rows, "head", scatter_dimension=1, tiled=True).astype(jnp.bfloat16)


def solution(mesh):
    return jax.shard_map(
        per_device,
        mesh=mesh,
        in_specs=(
            P(("groups", "ctx"), "head", None),
            P(("groups", "ctx"), "head", None),
            P(("groups", "ctx"), None),
            P(("groups", "ctx"), None),
            P("head", "ctx", None),
            P("ctx", "head", None),
        ),
        out_specs=P(("groups", "ctx"), "head"),
        check_vma=False,
    )
```

```python
import functools

import jax
import jax.numpy as jnp
from jax import lax
from jax.experimental import pallas as pl
from jax.experimental.pallas import tpu as pltpu
from jax.sharding import PartitionSpec as P

ROPE = 64
NOPE = 128
SCALE = (NOPE + ROPE) ** (-0.5)
F32 = jnp.float32
BF16 = jnp.bfloat16
MESH = pl.DeviceIdType.MESH
PIECES = 4
STAT = 16


def contract(a, b, da, db):
    return lax.dot_general(a, b, (((da,), (db,)), ((), ())), preferred_element_type=F32)


def far_first(n):
    return sorted(range(1, n), key=lambda d: abs(d - n // 2))


def kernel(
    n, ql, qr, cl, cr, vu, wo, out,
    qlb, qrb, clb, crb, clt, vub, vut, wob,
    lat_send, lat_recv, pr_send, pr_recv, att, at_send, at_recv,
    local_sem, q_send, q_recv, c_send, c_recv, s_send, s_recv, l_send, l_recv, p_send, p_recv, a_send, a_recv,
):
    me = lax.axis_index("ctx")
    hd = lax.axis_index("head")
    half = n // 2
    z = me // 2
    x = me % 2
    partner = 2 * z + 1 - x
    heads = ql.shape[1]
    tokens = cl.shape[0]
    share = vu.shape[1]
    cols = lat_send.shape[2]
    vshare = pr_send.shape[1]
    rows = pr_send.shape[2]
    chunks = out.shape[1] // 128
    pad = at_send.shape[2]

    own = pl.ds(0, tokens)
    local = [
        pltpu.make_async_copy(cl, clb.at[own], local_sem.at[0]),
        pltpu.make_async_copy(cr, crb.at[:, own], local_sem.at[1]),
        pltpu.make_async_copy(ql.at[0], qlb.at[z], local_sem.at[2]),
        pltpu.make_async_copy(qr.at[0], qrb.at[z], local_sem.at[3]),
        pltpu.make_async_copy(vu, vub, local_sem.at[4]),
        pltpu.make_async_copy(wo, wob, local_sem.at[5]),
    ]
    for copy in local:
        copy.start()

    barrier = pltpu.get_barrier_semaphore()
    line = [2 * ((z + d) % half) + x for d in far_first(half)]
    for peer in line:
        pl.semaphore_signal(barrier, inc=1, device_id={"ctx": peer}, device_id_type=MESH)
    pl.semaphore_signal(barrier, inc=1, device_id={"ctx": partner}, device_id_type=MESH)
    pl.semaphore_signal(barrier, inc=1, device_id={"head": 1 - hd}, device_id_type=MESH)
    pl.semaphore_wait(barrier, len(line) + 2)

    part = tokens // 2
    piece = part // PIECES
    spans = [(cr.at[:, pl.ds(pl.multiple_of(hd * part, part), part)],
              crb.at[:, pl.ds(pl.multiple_of(tokens + hd * part, part), part)])]
    for k in range(PIECES):
        spans.append((
            cl.at[pl.ds(pl.multiple_of(hd * part + k * piece, piece), piece)],
            clb.at[pl.ds(pl.multiple_of(tokens + hd * part + k * piece, piece), piece)],
        ))
    cache = [
        pltpu.make_async_remote_copy(
            src, dst, c_send.at[k], c_recv.at[k], device_id={"ctx": partner}, device_id_type=MESH
        )
        for k, (src, dst) in enumerate(spans)
    ]
    queries = []
    for d, peer in enumerate(line):
        for k, (src, dst) in enumerate(((ql, qlb), (qr, qrb))):
            queries.append(
                pltpu.make_async_remote_copy(
                    src.at[0], dst.at[z], q_send.at[k, d], q_recv.at[k, d],
                    device_id={"ctx": peer}, device_id_type=MESH,
                )
            )
    for copy in queries + cache:
        copy.start()

    for copy in local[:5]:
        copy.wait()
    clt[...] = clb[0:tokens].T
    vut[...] = vub[...].reshape(heads * share, vut.shape[0]).T

    swap = []
    for k, (_, dst) in enumerate(spans):
        cache[k].wait_recv()
        copy = pltpu.make_async_remote_copy(
            dst, dst, s_send.at[k], s_recv.at[k], device_id={"head": 1 - hd}, device_id_type=MESH
        )
        copy.start()
        swap.append(copy)
    for copy in queries:
        copy.wait_recv()

    q = qlb[...].reshape(cols, qlb.shape[2])
    r = qrb[...].reshape(cols, qrb.shape[2])
    first = contract(clb[0:tokens], q, 1, 1) + contract(crb[:, 0:tokens], r, 0, 1)
    for copy in swap:
        copy.wait_recv()
    second = contract(clb[tokens : 2 * tokens], q, 1, 1) + contract(crb[:, tokens : 2 * tokens], r, 0, 1)
    scores = jnp.concatenate([first, second], axis=0) * SCALE
    peak = jnp.max(scores, axis=0, keepdims=True).astype(BF16).astype(F32)
    raised = jnp.exp(scores - peak)
    total = jnp.sum(raised, axis=0, keepdims=True)
    weights = raised.astype(BF16)
    latent = contract(clt[...], weights[0:tokens], 1, 0) + contract(
        clb[tokens : 2 * tokens], weights[tokens : 2 * tokens], 0, 0
    )
    high = total.astype(BF16).astype(F32)
    row = lax.broadcasted_iota(jnp.int32, (STAT, cols), 0)
    stats = jnp.where(
        row == 0, peak, jnp.where(row == 1, high, jnp.where(row == 2, total - high, 0.0))
    ).astype(BF16)
    for j in range(n):
        lat_send[j, 0:share, :] = latent[j * share : (j + 1) * share].astype(BF16)
        lat_send[j, share : share + STAT, :] = stats

    def exchange(send, recv, send_sem, recv_sem):
        copies = []
        for d in far_first(n):
            peer = (me + d) % n
            copy = pltpu.make_async_remote_copy(
                send.at[peer], recv.at[me], send_sem.at[d], recv_sem.at[d],
                device_id={"ctx": peer}, device_id_type=MESH,
            )
            copy.start()
            copies.append(copy)
        recv[me] = send[me]
        for copy in copies:
            copy.wait_recv()
        return copies

    lat_copies = exchange(lat_send, lat_recv, l_send, l_recv)

    sides = []
    for side in range(2):
        blocks = [lat_recv[2 * k + side].astype(F32) for k in range(half)]
        peaks = [b[share : share + 1] for b in blocks]
        top = functools.reduce(jnp.maximum, peaks)
        factors = [jnp.exp(p - top) for p in peaks]
        whole = sum(f * (b[share + 1 : share + 2] + b[share + 2 : share + 3]) for f, b in zip(factors, blocks))
        sides.append(sum(f * b[0:share] for f, b in zip(factors, blocks)) / whole)
    comb = jnp.concatenate(sides, axis=1)

    per = max(256 // share, 1)
    stacked = jnp.concatenate([comb] * per, axis=0)
    lane = lax.broadcasted_iota(jnp.int32, stacked.shape, 1) % heads
    block = lax.broadcasted_iota(jnp.int32, stacked.shape, 0) // share
    flipped = jnp.zeros((vut.shape[0], rows), F32)
    for g in range(heads // per):
        rhs = jnp.where(lane == block + g * per, stacked, 0.0).astype(BF16)
        flipped += jnp.dot(
            vut[:, g * per * share : (g + 1) * per * share], rhs, preferred_element_type=F32
        )
    for j in range(n):
        pr_send[j] = flipped[j * vshare : (j + 1) * vshare].astype(BF16)
    pr_copies = exchange(pr_send, pr_recv, p_send, p_recv)

    head_out = sum(pr_recv[s].astype(F32) for s in range(n)).astype(BF16)
    wide = vshare * heads
    spread = (
        lax.broadcasted_iota(jnp.int32, (vshare, wide), 1) // heads
        == lax.broadcasted_iota(jnp.int32, (vshare, wide), 0)
    ).astype(F32).astype(BF16)
    copied = contract(head_out, spread, 0, 0)
    keep = (
        lax.broadcasted_iota(jnp.int32, (rows, wide), 1) % heads
        == lax.broadcasted_iota(jnp.int32, (rows, wide), 0) % heads
    )
    lhs = jnp.sum(jnp.where(keep, copied, 0.0).reshape(n, heads, wide), axis=1).astype(BF16)

    local[5].wait()
    step = 256 if chunks % 2 == 0 else 128
    at_copies = []
    for e in (1, 0):
        other = (hd + e) % 2
        for c in range(chunks * 128 // step):
            at = pl.multiple_of(other * chunks * 128 + c * step, 128)
            value = jnp.dot(lhs, wob[:, pl.ds(at, step)], preferred_element_type=F32)
            for t in range(step // 128):
                att[pl.ds(c * (step // 128) + t, n, stride=pad), :] = value[:, t * 128 : (t + 1) * 128]
        for c in range(chunks, pad):
            att[pl.ds(c, n, stride=pad), :] = jnp.zeros((n, 128), F32)
        for j in range(n):
            slot = (j % 2) * half + j // 2
            at_send[other, j] = att[slot * pad : (slot + 1) * pad, :].astype(BF16)
        for d in far_first(n) + [0] * e:
            peer = (me + d) % n
            copy = pltpu.make_async_remote_copy(
                at_send.at[other, peer], at_recv.at[hd, me], a_send.at[e, d], a_recv.at[e, d],
                device_id={"ctx": peer, "head": other}, device_id_type=MESH,
            )
            copy.start()
            at_copies.append(copy)
    at_recv[hd, me] = at_send[hd, me]
    for copy in at_copies:
        copy.wait_recv()
    result = sum(at_recv[k, s].astype(F32) for k in range(2) for s in range(n)).astype(BF16)
    for c in range(chunks):
        out[0:1, c * 128 : (c + 1) * 128] = result[c : c + 1, :]

    for copy in cache + queries + swap + lat_copies + pr_copies + at_copies:
        copy.wait_send()


def fused(n, query_latent, query_rope, cache_latent, cache_rope, value_up, out_proj):
    heads, latent_width = query_latent.shape[1:]
    rotary = query_rope.shape[2]
    tokens = cache_latent.shape[0]
    share, value_width = value_up.shape[1:]
    vshare, _, width = out_proj.shape
    half = n // 2
    cols = half * heads
    rows = n * heads
    mine = width // 2
    pad = -(-(mine // 128) // 16) * 16
    wide = vshare * heads
    dma = pltpu.SemaphoreType.DMA
    any_spec = pl.BlockSpec(memory_space=pl.ANY)
    return pl.pallas_call(
        functools.partial(kernel, n),
        out_shape=jax.ShapeDtypeStruct((1, mine), BF16),
        in_specs=[any_spec] * 6,
        out_specs=pl.BlockSpec(memory_space=pltpu.VMEM),
        scratch_shapes=[
            pltpu.VMEM((half, heads, latent_width), BF16),
            pltpu.VMEM((half, heads, rotary), BF16),
            pltpu.VMEM((2 * tokens, latent_width), BF16),
            pltpu.VMEM((rotary, 2 * tokens), BF16),
            pltpu.VMEM((latent_width, tokens), BF16),
            pltpu.VMEM(value_up.shape, BF16),
            pltpu.VMEM((value_width, heads * share), BF16),
            pltpu.VMEM((wide, width), BF16),
            pltpu.VMEM((n, share + STAT, cols), BF16),
            pltpu.VMEM((n, share + STAT, cols), BF16),
            pltpu.VMEM((n, vshare, rows), BF16),
            pltpu.VMEM((n, vshare, rows), BF16),
            pltpu.VMEM((n * pad, 128), F32),
            pltpu.VMEM((2, n, pad, 128), BF16),
            pltpu.VMEM((2, n, pad, 128), BF16),
            dma((6,)),
            dma((2, half)), dma((2, half)),
            dma((PIECES + 1,)), dma((PIECES + 1,)),
            dma((PIECES + 1,)), dma((PIECES + 1,)),
            dma((n,)), dma((n,)),
            dma((n,)), dma((n,)),
            dma((2, n)), dma((2, n)),
        ],
        compiler_params=pltpu.CompilerParams(
            collective_id=0, has_side_effects=True, vmem_limit_bytes=56 * 2**20
        ),
    )(query_latent, query_rope, cache_latent, cache_rope.T, value_up, out_proj.reshape(wide, width))


def per_device(query_latent, query_rope, cache_latent, cache_rope, value_up, out_proj):
    n = lax.axis_size("ctx")
    if n % 2 == 0 and n <= 16 and value_up.shape[1] % 16 == 0 and out_proj.shape[0] % 16 == 0:
        return fused(n, query_latent, query_rope, cache_latent, cache_rope, value_up, out_proj)
    return plain(query_latent, query_rope, cache_latent, cache_rope, value_up, out_proj)


def plain(query_latent, query_rope, cache_latent, cache_rope, value_up, out_proj):
    score_scale = (NOPE + ROPE) ** (-0.5)
    rows_here, heads_here, latent_width = query_latent.shape
    rotary_width = query_rope.shape[2]
    latent_share, value_width = (value_up.shape[1], value_up.shape[2])
    column_share = out_proj.shape[0]
    per_block = min(8, heads_here)
    block_count = heads_here // per_block
    latent_blocks = jnp.transpose(
        query_latent.reshape(rows_here, block_count, per_block, latent_width), (1, 0, 2, 3)
    )
    rotary_blocks = jnp.transpose(
        query_rope.reshape(rows_here, block_count, per_block, rotary_width), (1, 0, 2, 3)
    )
    value_blocks = value_up.reshape(block_count, per_block, latent_share, value_width)
    column_start = lax.axis_index("ctx") * column_share

    def attend_block(blocks):
        latent_block, rotary_block, value_block = blocks
        gathered_latent, gathered_rotary = (
            lax.all_gather(latent_block, "ctx", axis=0, tiled=True),
            lax.all_gather(rotary_block, "ctx", axis=0, tiled=True),
        )
        scores = (
            jnp.einsum(
                "qhc,kc->qhk", gathered_latent, cache_latent, preferred_element_type=jnp.float32
            )
            + jnp.einsum(
                "qhr,kr->qhk", gathered_rotary, cache_rope, preferred_element_type=jnp.float32
            )
        ) * score_scale
        peaks = jnp.max(scores, axis=2)
        raised = jnp.exp(scores - peaks[:, :, None])
        totals = jnp.sum(raised, axis=2)
        weights = raised.astype(jnp.bfloat16)
        latent_out = jnp.einsum(
            "qhk,kc->qhc", weights, cache_latent, preferred_element_type=jnp.float32
        )
        projected = jnp.einsum(
            "qhc,hcv->qhv",
            latent_out,
            lax.all_gather(value_block, "ctx", axis=1, tiled=True).astype(jnp.float32),
            precision=lax.Precision.HIGHEST,
        )
        peak_all = lax.pmax(peaks, "ctx")
        factor = jnp.exp(peaks - peak_all)
        total_all = lax.psum(totals * factor, "ctx")
        scaled = projected * (factor / total_all)[:, :, None]
        head_full = lax.psum(scaled, "ctx").astype(jnp.bfloat16)
        return lax.dynamic_slice_in_dim(head_full, column_start, column_share, 2)

    column_blocks = lax.map(attend_block, (latent_blocks, rotary_blocks, value_blocks))
    every_row = column_blocks.shape[1]
    head_cols = jnp.transpose(column_blocks, (1, 0, 2, 3)).reshape(
        every_row, heads_here, column_share
    )
    own_rows = lax.psum_scatter(
        jnp.einsum("qhv,vhd->qd", head_cols, out_proj, preferred_element_type=jnp.float32),
        "ctx",
        scatter_dimension=0,
        tiled=True,
    )
    return lax.psum_scatter(own_rows, "head", scatter_dimension=1, tiled=True).astype(jnp.bfloat16)


def solution(mesh):
    return jax.shard_map(
        per_device,
        mesh=mesh,
        in_specs=(
            P(("groups", "ctx"), "head", None),
            P(("groups", "ctx"), "head", None),
            P(("groups", "ctx"), None),
            P(("groups", "ctx"), None),
            P("head", "ctx", None),
            P("ctx", "head", None),
        ),
        out_specs=P(("groups", "ctx"), "head"),
        check_vma=False,
    )
```

```python
import functools

import jax
import jax.numpy as jnp
from jax import lax
from jax.experimental import pallas as pl
from jax.experimental.pallas import tpu as pltpu
from jax.sharding import PartitionSpec as P

ROPE = 64
NOPE = 128
SCALE = (NOPE + ROPE) ** (-0.5)
F32 = jnp.float32
BF16 = jnp.bfloat16
MESH = pl.DeviceIdType.MESH
PIECES = 4
STAT = 16


def mod(a, b):
    return a & (b - 1) if b & (b - 1) == 0 else a % b


def div(a, b):
    return a >> (b.bit_length() - 1) if b & (b - 1) == 0 else a // b


def contract(a, b, da, db):
    return lax.dot_general(a, b, (((da,), (db,)), ((), ())), preferred_element_type=F32)


def kernel(
    n, ql, qr, cl, cr, vu, wo, out,
    qlb, qrb, clb, crb, clt, vub, vut, wob,
    lat_send, lat_recv, pr_send, pr_recv, att, at_send, at_recv,
    local_sem, q_send, q_recv, c_send, c_recv, s_send, s_recv, l_send, l_recv, p_send, p_recv, a_send, a_recv,
):
    me = lax.axis_index("ctx")
    hd = lax.axis_index("head")
    half = n // 2
    z = me // 2
    x = me % 2
    partner = 2 * z + 1 - x
    heads = ql.shape[1]
    tokens = cl.shape[0]
    share = vu.shape[1]
    cols = lat_send.shape[2]
    vshare = pr_send.shape[1]
    rows = pr_send.shape[2]
    chunks = out.shape[1] // 128
    pad = at_send.shape[2]

    own = pl.ds(0, tokens)
    local = [
        pltpu.make_async_copy(cl, clb.at[own], local_sem.at[0]),
        pltpu.make_async_copy(cr, crb.at[:, own], local_sem.at[1]),
        pltpu.make_async_copy(ql.at[0], qlb.at[z], local_sem.at[2]),
        pltpu.make_async_copy(qr.at[0], qrb.at[z], local_sem.at[3]),
        pltpu.make_async_copy(vu, vub, local_sem.at[4]),
        pltpu.make_async_copy(wo, wob, local_sem.at[5]),
    ]
    for copy in local:
        copy.start()

    barrier = pltpu.get_barrier_semaphore()
    line = [2 * ((z + d) % half) + x for d in range(1, half)]
    for peer in line:
        pl.semaphore_signal(barrier, inc=1, device_id={"ctx": peer}, device_id_type=MESH)
    pl.semaphore_signal(barrier, inc=1, device_id={"ctx": partner}, device_id_type=MESH)
    pl.semaphore_signal(barrier, inc=1, device_id={"head": 1 - hd}, device_id_type=MESH)
    pl.semaphore_wait(barrier, len(line) + 2)

    part = tokens // 2
    piece = part // PIECES
    spans = [(cr.at[:, pl.ds(pl.multiple_of(hd * part, part), part)],
              crb.at[:, pl.ds(pl.multiple_of(tokens + hd * part, part), part)])]
    for k in range(PIECES):
        spans.append((
            cl.at[pl.ds(pl.multiple_of(hd * part + k * piece, piece), piece)],
            clb.at[pl.ds(pl.multiple_of(tokens + hd * part + k * piece, piece), piece)],
        ))
    cache = [
        pltpu.make_async_remote_copy(
            src, dst, c_send.at[k], c_recv.at[k], device_id={"ctx": partner}, device_id_type=MESH
        )
        for k, (src, dst) in enumerate(spans)
    ]
    queries = []
    for d, peer in enumerate(line):
        for k, (src, dst) in enumerate(((ql, qlb), (qr, qrb))):
            queries.append(
                pltpu.make_async_remote_copy(
                    src.at[0], dst.at[z], q_send.at[k, d], q_recv.at[k, d],
                    device_id={"ctx": peer}, device_id_type=MESH,
                )
            )
    for copy in queries + cache:
        copy.start()

    for copy in local[:5]:
        copy.wait()
    clt[...] = clb[0:tokens].T
    vut[...] = vub[...].reshape(heads * share, vut.shape[0]).T

    swap = []
    for k, (_, dst) in enumerate(spans):
        cache[k].wait_recv()
        copy = pltpu.make_async_remote_copy(
            dst, dst, s_send.at[k], s_recv.at[k], device_id={"head": 1 - hd}, device_id_type=MESH
        )
        copy.start()
        swap.append(copy)
    for copy in queries:
        copy.wait_recv()

    q = qlb[...].reshape(cols, qlb.shape[2])
    r = qrb[...].reshape(cols, qrb.shape[2])
    first = contract(clb[0:tokens], q, 1, 1) + contract(crb[:, 0:tokens], r, 0, 1)
    for copy in swap:
        copy.wait_recv()
    second = contract(clb[tokens : 2 * tokens], q, 1, 1) + contract(crb[:, tokens : 2 * tokens], r, 0, 1)
    scores = jnp.concatenate([first, second], axis=0) * SCALE
    peak = jnp.max(scores, axis=0, keepdims=True).astype(BF16).astype(F32)
    raised = jnp.exp(scores - peak)
    total = jnp.sum(raised, axis=0, keepdims=True)
    weights = raised.astype(BF16)
    latent = contract(clt[...], weights[0:tokens], 1, 0) + contract(
        clb[tokens : 2 * tokens], weights[tokens : 2 * tokens], 0, 0
    )
    high = total.astype(BF16).astype(F32)
    row = lax.broadcasted_iota(jnp.int32, (STAT, cols), 0)
    stats = jnp.where(
        row == 0, peak, jnp.where(row == 1, high, jnp.where(row == 2, total - high, 0.0))
    ).astype(BF16)
    for j in range(n):
        lat_send[j, 0:share, :] = latent[j * share : (j + 1) * share].astype(BF16)
        lat_send[j, share : share + STAT, :] = stats

    def exchange(send, recv, send_sem, recv_sem, earlier):
        copies = []
        for d in range(1, n):
            peer = (me + d) % n
            copy = pltpu.make_async_remote_copy(
                send.at[peer], recv.at[me], send_sem.at[d], recv_sem.at[d],
                device_id={"ctx": peer}, device_id_type=MESH,
            )
            copy.start()
            copies.append(copy)
        recv[me] = send[me]
        for copy in earlier:
            copy.wait_send()
        for copy in copies:
            copy.wait_recv()
        return copies

    lat_copies = exchange(lat_send, lat_recv, l_send, l_recv, queries + cache + swap)

    sides = []
    for side in range(2):
        blocks = [lat_recv[2 * k + side].astype(F32) for k in range(half)]
        peaks = [b[share : share + 1] for b in blocks]
        top = functools.reduce(jnp.maximum, peaks)
        factors = [jnp.exp(p - top) for p in peaks]
        whole = sum(f * (b[share + 1 : share + 2] + b[share + 2 : share + 3]) for f, b in zip(factors, blocks))
        sides.append(sum(f * b[0:share] for f, b in zip(factors, blocks)) / whole)
    comb = jnp.concatenate(sides, axis=1)

    per = max(256 // share, 1)
    stacked = jnp.concatenate([comb] * per, axis=0)
    lane = mod(lax.broadcasted_iota(jnp.int32, stacked.shape, 1), heads)
    block = div(lax.broadcasted_iota(jnp.int32, stacked.shape, 0), share)
    ahead = lane - block
    flipped = jnp.zeros((vut.shape[0], rows), F32)
    for g in range(heads // per):
        rhs = jnp.where(ahead == g * per, stacked, 0.0).astype(BF16)
        flipped += jnp.dot(
            vut[:, g * per * share : (g + 1) * per * share], rhs, preferred_element_type=F32
        )
    for j in range(n):
        pr_send[j] = flipped[j * vshare : (j + 1) * vshare].astype(BF16)
    pr_copies = exchange(pr_send, pr_recv, p_send, p_recv, lat_copies)

    head_out = sum(pr_recv[s].astype(F32) for s in range(n)).astype(BF16)
    wide = vshare * heads
    spread = (
        div(lax.broadcasted_iota(jnp.int32, (vshare, wide), 1), heads)
        == lax.broadcasted_iota(jnp.int32, (vshare, wide), 0)
    ).astype(F32).astype(BF16)
    copied = contract(head_out, spread, 0, 0)
    apart = lax.broadcasted_iota(jnp.int32, (rows, wide), 1) - lax.broadcasted_iota(
        jnp.int32, (rows, wide), 0
    )
    keep = mod(apart, heads) == 0
    lhs = jnp.sum(jnp.where(keep, copied, 0.0).reshape(n, heads, wide), axis=1).astype(BF16)

    local[5].wait()
    step = 256 if chunks % 2 == 0 else 128
    at_copies = []
    for e in (0, 1):
        other = (hd + e) % 2
        for c in range(chunks * 128 // step):
            at = pl.multiple_of(other * chunks * 128 + c * step, 128)
            value = jnp.dot(lhs, wob[:, pl.ds(at, step)], preferred_element_type=F32)
            for t in range(step // 128):
                att[pl.ds(c * (step // 128) + t, n, stride=pad), :] = value[:, t * 128 : (t + 1) * 128]
        for c in range(chunks, pad):
            att[pl.ds(c, n, stride=pad), :] = jnp.zeros((n, 128), F32)
        for j in range(n):
            slot = (j % 2) * half + j // 2
            at_send[other, j] = att[slot * pad : (slot + 1) * pad, :].astype(BF16)
        for d in [*range(1, n)] + [0] * e:
            peer = (me + d) % n
            copy = pltpu.make_async_remote_copy(
                at_send.at[other, peer], at_recv.at[hd, me], a_send.at[e, d], a_recv.at[e, d],
                device_id={"ctx": peer, "head": other}, device_id_type=MESH,
            )
            copy.start()
            at_copies.append(copy)
    at_recv[hd, me] = at_send[hd, me]
    for copy in pr_copies:
        copy.wait_send()
    for copy in at_copies:
        copy.wait_recv()
    result = sum(at_recv[k, s].astype(F32) for k in range(2) for s in range(n)).astype(BF16)
    for c in range(chunks):
        out[0:1, c * 128 : (c + 1) * 128] = result[c : c + 1, :]

    for copy in at_copies:
        copy.wait_send()


def fused(n, query_latent, query_rope, cache_latent, cache_rope, value_up, out_proj):
    heads, latent_width = query_latent.shape[1:]
    rotary = query_rope.shape[2]
    tokens = cache_latent.shape[0]
    share, value_width = value_up.shape[1:]
    vshare, _, width = out_proj.shape
    half = n // 2
    cols = half * heads
    rows = n * heads
    mine = width // 2
    pad = -(-(mine // 128) // 16) * 16
    wide = vshare * heads
    dma = pltpu.SemaphoreType.DMA
    any_spec = pl.BlockSpec(memory_space=pl.ANY)
    return pl.pallas_call(
        functools.partial(kernel, n),
        out_shape=jax.ShapeDtypeStruct((1, mine), BF16),
        in_specs=[any_spec] * 6,
        out_specs=pl.BlockSpec(memory_space=pltpu.VMEM),
        scratch_shapes=[
            pltpu.VMEM((half, heads, latent_width), BF16),
            pltpu.VMEM((half, heads, rotary), BF16),
            pltpu.VMEM((2 * tokens, latent_width), BF16),
            pltpu.VMEM((rotary, 2 * tokens), BF16),
            pltpu.VMEM((latent_width, tokens), BF16),
            pltpu.VMEM(value_up.shape, BF16),
            pltpu.VMEM((value_width, heads * share), BF16),
            pltpu.VMEM((wide, width), BF16),
            pltpu.VMEM((n, share + STAT, cols), BF16),
            pltpu.VMEM((n, share + STAT, cols), BF16),
            pltpu.VMEM((n, vshare, rows), BF16),
            pltpu.VMEM((n, vshare, rows), BF16),
            pltpu.VMEM((n * pad, 128), F32),
            pltpu.VMEM((2, n, pad, 128), BF16),
            pltpu.VMEM((2, n, pad, 128), BF16),
            dma((6,)),
            dma((2, half)), dma((2, half)),
            dma((PIECES + 1,)), dma((PIECES + 1,)),
            dma((PIECES + 1,)), dma((PIECES + 1,)),
            dma((n,)), dma((n,)),
            dma((n,)), dma((n,)),
            dma((2, n)), dma((2, n)),
        ],
        compiler_params=pltpu.CompilerParams(
            collective_id=0, has_side_effects=True, vmem_limit_bytes=56 * 2**20
        ),
    )(query_latent, query_rope, cache_latent, cache_rope.T, value_up, out_proj.reshape(wide, width))


def per_device(query_latent, query_rope, cache_latent, cache_rope, value_up, out_proj):
    n = lax.axis_size("ctx")
    if n % 2 == 0 and n <= 16 and value_up.shape[1] % 16 == 0 and out_proj.shape[0] % 16 == 0:
        return fused(n, query_latent, query_rope, cache_latent, cache_rope, value_up, out_proj)
    return plain(query_latent, query_rope, cache_latent, cache_rope, value_up, out_proj)


def plain(query_latent, query_rope, cache_latent, cache_rope, value_up, out_proj):
    score_scale = (NOPE + ROPE) ** (-0.5)
    rows_here, heads_here, latent_width = query_latent.shape
    rotary_width = query_rope.shape[2]
    latent_share, value_width = (value_up.shape[1], value_up.shape[2])
    column_share = out_proj.shape[0]
    per_block = min(8, heads_here)
    block_count = heads_here // per_block
    latent_blocks = jnp.transpose(
        query_latent.reshape(rows_here, block_count, per_block, latent_width), (1, 0, 2, 3)
    )
    rotary_blocks = jnp.transpose(
        query_rope.reshape(rows_here, block_count, per_block, rotary_width), (1, 0, 2, 3)
    )
    value_blocks = value_up.reshape(block_count, per_block, latent_share, value_width)
    column_start = lax.axis_index("ctx") * column_share

    def attend_block(blocks):
        latent_block, rotary_block, value_block = blocks
        gathered_latent, gathered_rotary = (
            lax.all_gather(latent_block, "ctx", axis=0, tiled=True),
            lax.all_gather(rotary_block, "ctx", axis=0, tiled=True),
        )
        scores = (
            jnp.einsum(
                "qhc,kc->qhk", gathered_latent, cache_latent, preferred_element_type=jnp.float32
            )
            + jnp.einsum(
                "qhr,kr->qhk", gathered_rotary, cache_rope, preferred_element_type=jnp.float32
            )
        ) * score_scale
        peaks = jnp.max(scores, axis=2)
        raised = jnp.exp(scores - peaks[:, :, None])
        totals = jnp.sum(raised, axis=2)
        weights = raised.astype(jnp.bfloat16)
        latent_out = jnp.einsum(
            "qhk,kc->qhc", weights, cache_latent, preferred_element_type=jnp.float32
        )
        projected = jnp.einsum(
            "qhc,hcv->qhv",
            latent_out,
            lax.all_gather(value_block, "ctx", axis=1, tiled=True).astype(jnp.float32),
            precision=lax.Precision.HIGHEST,
        )
        peak_all = lax.pmax(peaks, "ctx")
        factor = jnp.exp(peaks - peak_all)
        total_all = lax.psum(totals * factor, "ctx")
        scaled = projected * (factor / total_all)[:, :, None]
        head_full = lax.psum(scaled, "ctx").astype(jnp.bfloat16)
        return lax.dynamic_slice_in_dim(head_full, column_start, column_share, 2)

    column_blocks = lax.map(attend_block, (latent_blocks, rotary_blocks, value_blocks))
    every_row = column_blocks.shape[1]
    head_cols = jnp.transpose(column_blocks, (1, 0, 2, 3)).reshape(
        every_row, heads_here, column_share
    )
    own_rows = lax.psum_scatter(
        jnp.einsum("qhv,vhd->qd", head_cols, out_proj, preferred_element_type=jnp.float32),
        "ctx",
        scatter_dimension=0,
        tiled=True,
    )
    return lax.psum_scatter(own_rows, "head", scatter_dimension=1, tiled=True).astype(jnp.bfloat16)


def solution(mesh):
    return jax.shard_map(
        per_device,
        mesh=mesh,
        in_specs=(
            P(("groups", "ctx"), "head", None),
            P(("groups", "ctx"), "head", None),
            P(("groups", "ctx"), None),
            P(("groups", "ctx"), None),
            P("head", "ctx", None),
            P("ctx", "head", None),
        ),
        out_specs=P(("groups", "ctx"), "head"),
        check_vma=False,
    )
```

```python
import functools

import jax
import jax.numpy as jnp
from jax import lax
from jax.experimental import pallas as pl
from jax.experimental.pallas import tpu as pltpu
from jax.sharding import PartitionSpec as P

ROPE = 64
NOPE = 128
SCALE = (NOPE + ROPE) ** (-0.5)
F32 = jnp.float32
BF16 = jnp.bfloat16
MESH = pl.DeviceIdType.MESH
PIECES = 4
STAT = 16


def mod(a, b):
    return a & (b - 1) if b & (b - 1) == 0 else a % b


def div(a, b):
    return a >> (b.bit_length() - 1) if b & (b - 1) == 0 else a // b


def contract(a, b, da, db):
    return lax.dot_general(a, b, (((da,), (db,)), ((), ())), preferred_element_type=F32)


def kernel(
    n, ql, qr, cl, cr, vu, wo, out,
    qlb, qrb, clb, crb, clt, vub, vut, wob,
    lat_send, lat_recv, pr_send, pr_recv, att, at_send, at_recv,
    local_sem, q_send, q_recv, c_send, c_recv, s_send, s_recv, l_send, l_recv, p_send, p_recv, a_send, a_recv,
):
    me = lax.axis_index("ctx")
    hd = lax.axis_index("head")
    half = n // 2
    z = div(me, 2)
    x = mod(me, 2)
    partner = 2 * z + 1 - x
    heads = ql.shape[1]
    tokens = cl.shape[0]
    share = vu.shape[1]
    cols = lat_send.shape[2]
    vshare = pr_send.shape[1]
    rows = pr_send.shape[2]
    chunks = out.shape[1] // 128
    pad = at_send.shape[2]

    own = pl.ds(0, tokens)
    local = [
        pltpu.make_async_copy(cl, clb.at[own], local_sem.at[0]),
        pltpu.make_async_copy(cr, crb.at[:, own], local_sem.at[1]),
        pltpu.make_async_copy(ql.at[0], qlb.at[z], local_sem.at[2]),
        pltpu.make_async_copy(qr.at[0], qrb.at[z], local_sem.at[3]),
        pltpu.make_async_copy(vu, vub, local_sem.at[4]),
        pltpu.make_async_copy(wo, wob, local_sem.at[5]),
    ]
    for copy in local[:5]:
        copy.start()

    barrier = pltpu.get_barrier_semaphore()
    line = [2 * mod(z + d, half) + x for d in range(1, half)]
    for peer in line:
        pl.semaphore_signal(barrier, inc=1, device_id={"ctx": peer}, device_id_type=MESH)
    pl.semaphore_signal(barrier, inc=1, device_id={"ctx": partner}, device_id_type=MESH)
    pl.semaphore_signal(barrier, inc=1, device_id={"head": 1 - hd}, device_id_type=MESH)
    pl.semaphore_wait(barrier, len(line) + 2)

    part = tokens // 2
    piece = part // PIECES
    spans = [(cr.at[:, pl.ds(pl.multiple_of(hd * part, part), part)],
              crb.at[:, pl.ds(pl.multiple_of(tokens + hd * part, part), part)])]
    for k in range(PIECES):
        spans.append((
            cl.at[pl.ds(pl.multiple_of(hd * part + k * piece, piece), piece)],
            clb.at[pl.ds(pl.multiple_of(tokens + hd * part + k * piece, piece), piece)],
        ))
    cache = [
        pltpu.make_async_remote_copy(
            src, dst, c_send.at[k], c_recv.at[k], device_id={"ctx": partner}, device_id_type=MESH
        )
        for k, (src, dst) in enumerate(spans)
    ]
    queries = []
    for d, peer in enumerate(line):
        for k, (src, dst) in enumerate(((ql, qlb), (qr, qrb))):
            queries.append(
                pltpu.make_async_remote_copy(
                    src.at[0], dst.at[z], q_send.at[k, d], q_recv.at[k, d],
                    device_id={"ctx": peer}, device_id_type=MESH,
                )
            )
    for copy in queries + cache + local[5:]:
        copy.start()

    for copy in local[:5]:
        copy.wait()
    clt[...] = clb[0:tokens].T
    vut[...] = vub[...].reshape(heads * share, vut.shape[0]).T

    swap = []
    for k, (_, dst) in enumerate(spans):
        cache[k].wait_recv()
        copy = pltpu.make_async_remote_copy(
            dst, dst, s_send.at[k], s_recv.at[k], device_id={"head": 1 - hd}, device_id_type=MESH
        )
        copy.start()
        swap.append(copy)
    for copy in queries:
        copy.wait_recv()

    q = qlb[...].reshape(cols, qlb.shape[2])
    r = qrb[...].reshape(cols, qrb.shape[2])
    first = contract(clb[0:tokens], q, 1, 1) + contract(crb[:, 0:tokens], r, 0, 1)
    for copy in swap:
        copy.wait_recv()
    second = contract(clb[tokens : 2 * tokens], q, 1, 1) + contract(crb[:, tokens : 2 * tokens], r, 0, 1)
    scores = jnp.concatenate([first, second], axis=0) * SCALE
    peak = jnp.max(scores, axis=0, keepdims=True).astype(BF16).astype(F32)
    raised = jnp.exp(scores - peak)
    total = jnp.sum(raised, axis=0, keepdims=True)
    weights = raised.astype(BF16)
    latent = contract(clt[...], weights[0:tokens], 1, 0) + contract(
        clb[tokens : 2 * tokens], weights[tokens : 2 * tokens], 0, 0
    )
    high = total.astype(BF16).astype(F32)
    row = lax.broadcasted_iota(jnp.int32, (STAT, cols), 0)
    stats = jnp.where(
        row == 0, peak, jnp.where(row == 1, high, jnp.where(row == 2, total - high, 0.0))
    ).astype(BF16)
    for j in range(n):
        lat_send[j, 0:share, :] = latent[j * share : (j + 1) * share].astype(BF16)
        lat_send[j, share : share + STAT, :] = stats

    def exchange(send, recv, send_sem, recv_sem, earlier):
        copies = []
        for d in [*range(1, n, 2), *range(2, n, 2)]:
            peer = mod(me + d, n)
            copy = pltpu.make_async_remote_copy(
                send.at[peer], recv.at[me], send_sem.at[d], recv_sem.at[d],
                device_id={"ctx": peer}, device_id_type=MESH,
            )
            copy.start()
            copies.append(copy)
        recv[me] = send[me]
        for copy in earlier:
            copy.wait_send()
        for copy in copies:
            copy.wait_recv()
        return copies

    lat_copies = exchange(lat_send, lat_recv, l_send, l_recv, queries + cache + swap)

    sides = []
    for side in range(2):
        blocks = [lat_recv[2 * k + side].astype(F32) for k in range(half)]
        peaks = [b[share : share + 1] for b in blocks]
        top = functools.reduce(jnp.maximum, peaks)
        factors = [jnp.exp(p - top) for p in peaks]
        whole = sum(f * (b[share + 1 : share + 2] + b[share + 2 : share + 3]) for f, b in zip(factors, blocks))
        sides.append(sum(f * b[0:share] for f, b in zip(factors, blocks)) / whole)
    comb = jnp.concatenate(sides, axis=1)

    per = max(256 // share, 1)
    stacked = jnp.concatenate([comb.astype(BF16)] * per, axis=0)
    lane = mod(lax.broadcasted_iota(jnp.int32, stacked.shape, 1), heads)
    block = div(lax.broadcasted_iota(jnp.int32, stacked.shape, 0), share)
    ahead = lane - block
    flipped = jnp.zeros((vut.shape[0], rows), F32)
    for g in range(heads // per):
        rhs = jnp.where(ahead == g * per, stacked, jnp.zeros((), BF16))
        flipped += jnp.dot(
            vut[:, g * per * share : (g + 1) * per * share], rhs, preferred_element_type=F32
        )
    for j in range(n):
        pr_send[j] = flipped[j * vshare : (j + 1) * vshare].astype(BF16)
    pr_copies = exchange(pr_send, pr_recv, p_send, p_recv, lat_copies)

    head_out = sum(pr_recv[s].astype(F32) for s in range(n)).astype(BF16)
    wide = vshare * heads
    spread = (
        div(lax.broadcasted_iota(jnp.int32, (vshare, wide), 1), heads)
        == lax.broadcasted_iota(jnp.int32, (vshare, wide), 0)
    ).astype(F32).astype(BF16)
    copied = contract(head_out, spread, 0, 0)
    apart = lax.broadcasted_iota(jnp.int32, (rows, wide), 1) - lax.broadcasted_iota(
        jnp.int32, (rows, wide), 0
    )
    keep = mod(apart, heads) == 0
    lhs = jnp.sum(jnp.where(keep, copied, 0.0).reshape(n, heads, wide), axis=1).astype(BF16)

    local[5].wait()
    step = 256 if chunks % 2 == 0 else 128
    at_copies = []
    for e in (0, 1):
        other = mod(hd + e, 2)
        for c in range(chunks * 128 // step):
            at = pl.multiple_of(other * chunks * 128 + c * step, 128)
            value = jnp.dot(lhs, wob[:, pl.ds(at, step)], preferred_element_type=F32)
            for t in range(step // 128):
                att[pl.ds(c * (step // 128) + t, n, stride=pad), :] = value[:, t * 128 : (t + 1) * 128]
        for c in range(chunks, pad):
            att[pl.ds(c, n, stride=pad), :] = jnp.zeros((n, 128), F32)
        for j in range(n):
            slot = (j % 2) * half + j // 2
            at_send[other, j] = att[slot * pad : (slot + 1) * pad, :].astype(BF16)
        for d in [*range(1, n)] + [0] * e:
            peer = mod(me + d, n)
            copy = pltpu.make_async_remote_copy(
                at_send.at[other, peer], at_recv.at[hd, me], a_send.at[e, d], a_recv.at[e, d],
                device_id={"ctx": peer, "head": other}, device_id_type=MESH,
            )
            copy.start()
            at_copies.append(copy)
    at_recv[hd, me] = at_send[hd, me]
    for copy in pr_copies:
        copy.wait_send()
    for copy in at_copies:
        copy.wait_recv()
    result = sum(at_recv[k, s].astype(F32) for k in range(2) for s in range(n)).astype(BF16)
    for c in range(chunks):
        out[0:1, c * 128 : (c + 1) * 128] = result[c : c + 1, :]

    for copy in at_copies:
        copy.wait_send()


def fused(n, query_latent, query_rope, cache_latent, cache_rope, value_up, out_proj):
    heads, latent_width = query_latent.shape[1:]
    rotary = query_rope.shape[2]
    tokens = cache_latent.shape[0]
    share, value_width = value_up.shape[1:]
    vshare, _, width = out_proj.shape
    half = n // 2
    cols = half * heads
    rows = n * heads
    mine = width // 2
    pad = -(-(mine // 128) // 16) * 16
    wide = vshare * heads
    dma = pltpu.SemaphoreType.DMA
    any_spec = pl.BlockSpec(memory_space=pl.ANY)
    return pl.pallas_call(
        functools.partial(kernel, n),
        out_shape=jax.ShapeDtypeStruct((1, mine), BF16),
        in_specs=[any_spec] * 6,
        out_specs=pl.BlockSpec(memory_space=pltpu.VMEM),
        scratch_shapes=[
            pltpu.VMEM((half, heads, latent_width), BF16),
            pltpu.VMEM((half, heads, rotary), BF16),
            pltpu.VMEM((2 * tokens, latent_width), BF16),
            pltpu.VMEM((rotary, 2 * tokens), BF16),
            pltpu.VMEM((latent_width, tokens), BF16),
            pltpu.VMEM(value_up.shape, BF16),
            pltpu.VMEM((value_width, heads * share), BF16),
            pltpu.VMEM((wide, width), BF16),
            pltpu.VMEM((n, share + STAT, cols), BF16),
            pltpu.VMEM((n, share + STAT, cols), BF16),
            pltpu.VMEM((n, vshare, rows), BF16),
            pltpu.VMEM((n, vshare, rows), BF16),
            pltpu.VMEM((n * pad, 128), F32),
            pltpu.VMEM((2, n, pad, 128), BF16),
            pltpu.VMEM((2, n, pad, 128), BF16),
            dma((6,)),
            dma((2, half)), dma((2, half)),
            dma((PIECES + 1,)), dma((PIECES + 1,)),
            dma((PIECES + 1,)), dma((PIECES + 1,)),
            dma((n,)), dma((n,)),
            dma((n,)), dma((n,)),
            dma((2, n)), dma((2, n)),
        ],
        compiler_params=pltpu.CompilerParams(
            collective_id=0, has_side_effects=True, vmem_limit_bytes=56 * 2**20
        ),
    )(query_latent, query_rope, cache_latent, cache_rope.T, value_up, out_proj.reshape(wide, width))


def per_device(query_latent, query_rope, cache_latent, cache_rope, value_up, out_proj):
    n = lax.axis_size("ctx")
    if n % 2 == 0 and n <= 16 and value_up.shape[1] % 16 == 0 and out_proj.shape[0] % 16 == 0:
        return fused(n, query_latent, query_rope, cache_latent, cache_rope, value_up, out_proj)
    return plain(query_latent, query_rope, cache_latent, cache_rope, value_up, out_proj)


def plain(query_latent, query_rope, cache_latent, cache_rope, value_up, out_proj):
    score_scale = (NOPE + ROPE) ** (-0.5)
    rows_here, heads_here, latent_width = query_latent.shape
    rotary_width = query_rope.shape[2]
    latent_share, value_width = (value_up.shape[1], value_up.shape[2])
    column_share = out_proj.shape[0]
    per_block = min(8, heads_here)
    block_count = heads_here // per_block
    latent_blocks = jnp.transpose(
        query_latent.reshape(rows_here, block_count, per_block, latent_width), (1, 0, 2, 3)
    )
    rotary_blocks = jnp.transpose(
        query_rope.reshape(rows_here, block_count, per_block, rotary_width), (1, 0, 2, 3)
    )
    value_blocks = value_up.reshape(block_count, per_block, latent_share, value_width)
    column_start = lax.axis_index("ctx") * column_share

    def attend_block(blocks):
        latent_block, rotary_block, value_block = blocks
        gathered_latent, gathered_rotary = (
            lax.all_gather(latent_block, "ctx", axis=0, tiled=True),
            lax.all_gather(rotary_block, "ctx", axis=0, tiled=True),
        )
        scores = (
            jnp.einsum(
                "qhc,kc->qhk", gathered_latent, cache_latent, preferred_element_type=jnp.float32
            )
            + jnp.einsum(
                "qhr,kr->qhk", gathered_rotary, cache_rope, preferred_element_type=jnp.float32
            )
        ) * score_scale
        peaks = jnp.max(scores, axis=2)
        raised = jnp.exp(scores - peaks[:, :, None])
        totals = jnp.sum(raised, axis=2)
        weights = raised.astype(jnp.bfloat16)
        latent_out = jnp.einsum(
            "qhk,kc->qhc", weights, cache_latent, preferred_element_type=jnp.float32
        )
        projected = jnp.einsum(
            "qhc,hcv->qhv",
            latent_out,
            lax.all_gather(value_block, "ctx", axis=1, tiled=True).astype(jnp.float32),
            precision=lax.Precision.HIGHEST,
        )
        peak_all = lax.pmax(peaks, "ctx")
        factor = jnp.exp(peaks - peak_all)
        total_all = lax.psum(totals * factor, "ctx")
        scaled = projected * (factor / total_all)[:, :, None]
        head_full = lax.psum(scaled, "ctx").astype(jnp.bfloat16)
        return lax.dynamic_slice_in_dim(head_full, column_start, column_share, 2)

    column_blocks = lax.map(attend_block, (latent_blocks, rotary_blocks, value_blocks))
    every_row = column_blocks.shape[1]
    head_cols = jnp.transpose(column_blocks, (1, 0, 2, 3)).reshape(
        every_row, heads_here, column_share
    )
    own_rows = lax.psum_scatter(
        jnp.einsum("qhv,vhd->qd", head_cols, out_proj, preferred_element_type=jnp.float32),
        "ctx",
        scatter_dimension=0,
        tiled=True,
    )
    return lax.psum_scatter(own_rows, "head", scatter_dimension=1, tiled=True).astype(jnp.bfloat16)


def solution(mesh):
    return jax.shard_map(
        per_device,
        mesh=mesh,
        in_specs=(
            P(("groups", "ctx"), "head", None),
            P(("groups", "ctx"), "head", None),
            P(("groups", "ctx"), None),
            P(("groups", "ctx"), None),
            P("head", "ctx", None),
            P("ctx", "head", None),
        ),
        out_specs=P(("groups", "ctx"), "head"),
        check_vma=False,
    )
```
